512 devices in a mesh: dp: 64 (over z, y), mp: 8 (over x, core).
Axes of the slice: x: 4, y: 4, z: 16, core: 2. Of those that a mesh axis runs over, the one named last changes fastest.
Arguments:
- tokens: bfloat16 [16384, 1024], P('dp'), may hold values from -6 to 6
- cotangent: bfloat16 [16384, 1024], P('dp')
- gain: float32 [1024], replicated, may hold values from 0.5 to 1.5
- shift: float32 [1024], replicated, may hold values from -3 to 3
- w_in: bfloat16 [1024, 4096], P(None, 'mp')
- w_out: bfloat16 [4096, 1024], P('mp')
- noise_in: float32 [1024, 4096], P('dp', 'mp'), may hold values from -0.75 to 0.75
- noise_out: float32 [4096, 1024], P('mp', 'dp'), may hold values from -0.75 to 0.75
Outputs:
- input_grad: bfloat16 [16384, 1024], P('dp')
- update_in: float32 [1024, 4096], P('dp', 'mp')
- update_out: float32 [4096, 1024], P('mp', 'dp')
The draws below stay inside these ranges and needn't reach their ends.
All inputs are finite; a program needn't handle non-finite values.
Results may differ from the reference program's by a relative error of at most 0.018.
Values may be sent and summed in bfloat16 or wider, within the bound.
A program may use at most 64 MiB of HBM per device.

```python
import math
import jax
import jax.numpy as jnp
from jax import lax

D = 1024
FFW = 4096
SEQ = 256
IMAGES = 64
ROWS = 16384
N_MP = 8


def unit_values(key, shape):
    return jnp.clip(jax.random.normal(key, shape, jnp.float32), -4.0, 4.0)


def draw_cotangent(key, part):
    key = jax.random.fold_in(key, 7)
    order_key, jitter_key, shared_key, image_key, value_key = jax.random.split(key, 5)
    ranks = jax.random.permutation(order_key, IMAGES).astype(jnp.float32)
    jitter = jax.random.uniform(jitter_key, (IMAGES,), jnp.float32, 0.0, 1.0)
    position = (ranks + jitter) / float(IMAGES)
    low = math.log(0.05)
    high = math.log(5.0)
    scales = jnp.exp(low + (high - low) * position).reshape(IMAGES, 1, 1)
    shared = unit_values(shared_key, (1, 1, D))
    own = unit_values(image_key, (IMAGES, 1, D))
    values = unit_values(value_key, (IMAGES, SEQ, D))
    common = (shared + own) * math.sqrt(0.5)
    values = (common + values) * math.sqrt(0.5)
    values = values * scales * (1.0 / math.sqrt(SEQ))
    return values.reshape(IMAGES * SEQ, D).astype(jnp.bfloat16)


def column_scales(key, top):
    position = jnp.arange(FFW, dtype=jnp.float32) / float(FFW - 1)
    rough = jnp.exp(jax.random.uniform(key, (FFW,), jnp.float32, math.log(0.8), math.log(1.25)))
    return jnp.exp(math.log(top) * position) * rough


def draw_w_in(key, part):
    key = jax.random.fold_in(key, 11)
    scale_key, value_key = jax.random.split(key)
    scales = column_scales(scale_key, 3.0)
    values = jnp.clip(jax.random.normal(value_key, (D, FFW), jnp.float32), -4.0, 4.0)
    values = values * scales[None, :] * (0.5 / math.sqrt(D))
    return values.astype(jnp.bfloat16)


def draw_w_out(key, part):
    key = jax.random.fold_in(key, 13)
    scale_key, value_key = jax.random.split(key)
    top = 4.0
    values = jnp.clip(jax.random.normal(value_key, (FFW, D), jnp.float32), -4.0, 4.0)
    scales = column_scales(scale_key, top) / math.sqrt(top)
    values = values * scales[:, None] * (2.0 / math.sqrt(FFW))
    return values.astype(jnp.bfloat16)


def shard_levels(key, extent, shards, low, largest):
    def one(axis_at, parts):
        draws = jax.random.uniform(jax.random.fold_in(jax.random.fold_in(key, 6), axis_at), (parts,), jnp.float32, low / len(shards), largest / len(shards))
        return jnp.repeat(jnp.exp(draws), extent[axis_at] // parts).reshape((-1,) + (1,) * (len(extent) - axis_at - 1))

    loudness = one(*shards[0])
    for cut in shards[1:]:
        loudness = loudness * one(*cut)
    return loudness


def normal_values(key, shape, spread, reach, cuts=(), kind=jnp.bfloat16):
    values = jax.random.normal(key, shape, jnp.float32) * spread
    if len(cuts) > 0:
        values = shard_levels(key, shape, cuts, -0.22, 0.18) * values
    return jnp.clip(values, min=-reach, max=reach).astype(kind)


def setup_inputs(seed: int = 0) -> dict:
    arg_keys = jax.random.split(jax.random.key(seed), 9)
    tokens = normal_values(arg_keys[0], (ROWS, D), 1.0, 6.0, ((0, 64),))
    cotangent = draw_cotangent(jax.random.fold_in(arg_keys[8], 71), 0)
    gain = jnp.clip(1.0 + 0.1 * jax.random.normal(arg_keys[2], (D,), jnp.float32), 0.5, 1.5)
    shift = normal_values(arg_keys[3], (D,), 0.5, 3.0, (), jnp.float32)
    w_in = draw_w_in(jax.random.fold_in(arg_keys[8], 71), 0)
    w_out = draw_w_out(jax.random.fold_in(arg_keys[8], 71), 0)
    noise_in = normal_values(arg_keys[6], (D, FFW), 0.05, 0.75, ((0, 64), (1, 8)), jnp.float32)
    noise_out = normal_values(arg_keys[7], (FFW, D), 0.05, 0.75, ((0, 8), (1, 64)), jnp.float32)
    return dict(tokens=tokens, cotangent=cotangent, gain=gain, shift=shift, w_in=w_in, w_out=w_out, noise_in=noise_in, noise_out=noise_out)


def layer_normalize(tokens, gain, shift):
    values = tokens.astype(jnp.float32)
    centered_rows = values - lax.optimization_barrier(jnp.mean(values, axis=-1, keepdims=True))
    variance = lax.optimization_barrier(jnp.mean(centered_rows * centered_rows, axis=-1, keepdims=True))
    inverse_deviation = lax.rsqrt(variance + 1e-05)
    standardized_input = centered_rows * inverse_deviation
    normalized_rows = (standardized_input * gain + shift).astype(jnp.bfloat16)
    return (standardized_input, inverse_deviation, normalized_rows)

def gelu_parts(pre):
    cumul = 0.5 * (1.0 + lax.erf(pre * (1.0 / math.sqrt(2.0))))
    density = jnp.exp(-0.5 * pre * pre) * (1.0 / math.sqrt(2.0 * math.pi))
    return (pre * cumul, cumul + pre * density)

def reference(tokens, cotangent, gain, shift, w_in, w_out, noise_in, noise_out):
    standardized_input, inverse_deviation, normalized_rows = layer_normalize(tokens, gain, shift)
    pre = jnp.dot(normalized_rows, w_in, preferred_element_type=jnp.float32)
    act, slope = gelu_parts(pre)
    act = act.astype(jnp.bfloat16)
    back = lax.dot_general(cotangent, w_out, (((1,), (1,)), ((), ())), preferred_element_type=jnp.float32)
    grad_pre = (back * slope).astype(jnp.bfloat16)
    group = FFW // N_MP
    summed = jnp.zeros((tokens.shape[0], D), jnp.float32)
    for index in range(N_MP):
        part = lax.dot_general(grad_pre[:, index * group:(index + 1) * group], w_in[:, index * group:(index + 1) * group], (((1,), (1,)), ((), ())), preferred_element_type=jnp.float32)
        part = lax.optimization_barrier(part.astype(jnp.bfloat16))
        summed = summed + part.astype(jnp.float32)
    scaled_rows = summed * gain
    normed_difference = inverse_deviation * (scaled_rows - lax.optimization_barrier(jnp.mean(scaled_rows, axis=-1, keepdims=True)) - standardized_input * lax.optimization_barrier(jnp.mean(scaled_rows * standardized_input, axis=-1, keepdims=True)))
    input_grad = (cotangent.astype(jnp.float32) + normed_difference).astype(jnp.bfloat16)
    count = tokens.shape[0] // SEQ
    normed3 = normalized_rows.reshape(count, SEQ, D)
    act3 = act.reshape(count, SEQ, FFW)
    cot3 = cotangent.reshape(count, SEQ, D)
    grad3 = grad_pre.reshape(count, SEQ, FFW)

    def image_norm(item):
        hrows, arows, drows, grows = [piece.astype(jnp.float32) for piece in item]
        hp = lax.Precision.HIGHEST
        gram_h = jnp.dot(hrows, hrows.T, precision=hp)
        gram_g = jnp.dot(grows, grows.T, precision=hp)
        gram_a = jnp.dot(arows, arows.T, precision=hp)
        gram_d = jnp.dot(drows, drows.T, precision=hp)
        return jnp.sum(gram_h * gram_g) + jnp.sum(gram_a * gram_d)
    sq_norm = lax.map(image_norm, (normed3, act3, cot3, grad3))
    clip = jnp.minimum(1.0, float(D) / jnp.sqrt(sq_norm + 1e-06))

    def add_image(carry, item):
        hrows, grows, arows, drows, factor = item
        first = lax.dot_general(hrows, grows, (((0,), (0,)), ((), ())), preferred_element_type=jnp.float32)
        second = lax.dot_general(arows, drows, (((0,), (0,)), ((), ())), preferred_element_type=jnp.float32)
        return ((carry[0] + factor * first, carry[1] + factor * second), None)
    start = (jnp.zeros((D, FFW), jnp.float32), jnp.zeros((FFW, D), jnp.float32))
    (sum_in, sum_out), unused = lax.scan(add_image, start, (normed3, grad3, act3, cot3, clip))
    update_in = sum_in / float(count) + noise_in
    update_out = sum_out / float(count) + noise_out
    return (input_grad, update_in, update_out)
```

```python
import functools
import math

import jax
import jax.numpy as jnp
from jax import lax
from jax.experimental import pallas as pl
from jax.experimental.pallas import tpu as pltpu
from jax.sharding import PartitionSpec as P

MESH = pl.DeviceIdType.MESH
NY = 4
BF16, F32 = jnp.bfloat16, jnp.float32


def layer_normalize(tokens, gain, shift):
    values = tokens.astype(F32)
    centered_rows = values - jnp.mean(values, axis=-1, keepdims=True)
    variance = jnp.mean(centered_rows * centered_rows, axis=-1, keepdims=True)
    inverse_deviation = lax.rsqrt(variance + 1e-05)
    standardized_input = centered_rows * inverse_deviation
    normalized_rows = (standardized_input * gain + shift).astype(BF16)
    return standardized_input, inverse_deviation, normalized_rows


def gelu_parts(pre):
    cumul = 0.5 * (1.0 + lax.erf(pre * (1.0 / math.sqrt(2.0))))
    density = jnp.exp(-0.5 * pre * pre) * (1.0 / math.sqrt(2.0 * math.pi))
    return pre * cumul, cumul + pre * density


def dot(left, right, dims):
    return lax.dot_general(left, right, (dims, ((), ())), preferred_element_type=F32)


def kernel(
    nz, nmp, tok, cot, gain, shift, win, wout, nin, nout,
    ig, uin, uout,
    normed, act, grad, pre, back, pin, pout, part, nrm, xrs,
    s1, r1, s2, r2, zs, zr,
    n_send, n_recv, x_send, x_recv, g_send, g_recv,
    y1_send, y1_recv, y2_send, y2_recv, z_send, z_recv,
):
    seq, width = tok.shape
    group = win.shape[1]
    blk = width // (NY * nz)
    rows = seq // nmp
    images = float(nz * NY)
    half = nz // 2
    dp, mp = lax.axis_index("dp"), lax.axis_index("mp")
    z, y = lax.div(dp, NY), lax.rem(dp, NY)

    def at_y(step):
        return lax.rem(y + step + NY, NY)

    def at_z(step):
        return lax.rem(z + step + nz, nz)

    def at_mp(step):
        return lax.rem(mp + step, nmp)

    y_to = ((z * NY + at_y(1), mp), (z * NY + at_y(-1), mp))
    z_to = ((at_z(1) * NY + y, mp), (at_z(-1) * NY + y, mp))

    barrier = pltpu.get_barrier_semaphore()
    greeted = [*y_to, *z_to] + [(dp, at_mp(j)) for j in range(1, nmp)]
    for other in greeted:
        pl.semaphore_signal(barrier, inc=1, device_id=other, device_id_type=MESH)

    pending = []

    def send(src, dst, send_sem, recv_sem, to):
        copy = pltpu.make_async_remote_copy(
            src_ref=src, dst_ref=dst, send_sem=send_sem, recv_sem=recv_sem,
            device_id=to, device_id_type=MESH,
        )
        copy.start()
        pending.append(copy)
        return copy

    tile = min(seq, 32)

    def norm_tile(t, carry):
        at = pl.ds(pl.multiple_of(t * tile, tile), tile)
        normed[at, :] = layer_normalize(tok[at, :], gain[...], shift[...])[2]
        return carry

    lax.fori_loop(0, seq // tile, norm_tile, 0)
    pre[...] = dot(normed[...], win[...], ((1,), (0,)))
    back[...] = dot(cot[...], wout[...], ((1,), (1,)))

    def gelu_tile(t, carry):
        at = pl.ds(pl.multiple_of(t * tile, tile), tile)
        value, slope = gelu_parts(pre[at, :])
        act[at, :] = value.astype(BF16)
        grad[at, :] = (back[at, :] * slope).astype(BF16)
        return carry

    lax.fori_loop(0, seq // tile, gelu_tile, 0)

    step = min(width, 256)
    norm = jnp.zeros((8, 128), F32)
    for left, right, out in ((normed, grad, pin), (cot, act, pout)):
        for t in range(width // step):
            prod = dot(left[:, t * step : (t + 1) * step], right[...], ((0,), (0,)))
            out[t * step : (t + 1) * step, :] = prod
            square = jnp.sum((prod * prod).reshape(step // 8, 8, group), axis=0)
            for c in range(group // 128):
                norm = norm + square[:, c * 128 : (c + 1) * 128]
    nrm[0] = norm

    pl.semaphore_wait(barrier, len(greeted))
    n_copies = [
        send(nrm.at[0], nrm.at[j], n_send.at[j], n_recv.at[j], (dp, at_mp(j)))
        for j in range(1, nmp)
    ]

    part[...] = dot(grad[...], win[...], ((1,), (1,))).astype(BF16)
    x_copies = []
    for j in range(1, nmp):
        at = pl.ds(pl.multiple_of(at_mp(j) * rows, rows), rows)
        x_copies.append(
            send(part.at[at, :], xrs.at[j], x_send.at[j], x_recv.at[j], (dp, at_mp(j)))
        )

    for copy in n_copies:
        copy.wait_recv()
    total = jnp.sum(jnp.sum(nrm[...], axis=0), keepdims=True)
    clip = jnp.minimum(1.0, float(width) / jnp.sqrt(total + 1e-06))

    def mine(which, b, yy):
        at = pl.ds(pl.multiple_of((b * NY + yy) * blk, blk), blk)
        return which[at, :] * clip

    chunks, first = [], 0
    for k in range(half, -1, -1):
        steps = [k] if k in (0, half) else [k, -k]
        chunks.append((k, first, steps))
        first += len(steps)
    y1, y2, zc = {}, {}, {}

    def stage_a(i):
        k, o, steps = chunks[i]
        for t, st in enumerate(steps):
            b = at_z(st)
            s1[0, o + t] = mine(pin, b, at_y(2)).astype(BF16)
            s1[1, o + t] = mine(pout, b, at_y(2)).astype(BF16)
        at = pl.ds(o, len(steps))
        y1[i] = [
            send(s1.at[d, at], r1.at[d, at], y1_send.at[d, i], y1_recv.at[d, i], y_to[d])
            for d in range(2)
        ]

    def stage_b(i):
        k, o, steps = chunks[i]
        for copy in y1[i]:
            copy.wait_recv()
        for t, st in enumerate(steps):
            b, s = at_z(st), o + t
            s2[0, s, :blk] = (mine(pin, b, at_y(1)) + r1[0, s].astype(F32)).astype(BF16)
            s2[0, s, blk:] = mine(pout, b, at_y(1)).astype(BF16)
            s2[1, s, :blk] = mine(pin, b, at_y(-1)).astype(BF16)
            s2[1, s, blk:] = (mine(pout, b, at_y(-1)) + r1[1, s].astype(F32)).astype(BF16)
        at = pl.ds(o, len(steps))
        y2[i] = [
            send(s2.at[d, at], r2.at[d, at], y2_send.at[d, i], y2_recv.at[d, i], y_to[d])
            for d in range(2)
        ]

    def stage_c(i):
        k, o, steps = chunks[i]
        for copy in y2[i]:
            copy.wait_recv()
        sums = []
        for t, st in enumerate(steps):
            b, s = at_z(st), o + t
            sums.append([
                mine(which, b, y) + r2[0, s, at].astype(F32) + r2[1, s, at].astype(F32)
                for which, at in ((pin, slice(0, blk)), (pout, slice(blk, 2 * blk)))
            ])
        if i > 0:
            for copy in zc[i - 1]:
                copy.wait_recv()
        if k == half:
            for d in range(2):
                zs[d, i, :blk] = sums[0][d].astype(BF16)
            at = pl.ds(0, blk)
            zc[i] = [
                send(zs.at[d, i, at], zr.at[d, i, at], z_send.at[d, i], z_recv.at[d, i], z_to[d])
                for d in range(2)
            ]
            return
        for d in range(2):
            place = sums[d if k > 0 else 0]
            if k == half - 1:
                place[d] = place[d] + zr[d, i - 1, :blk].astype(F32)
            else:
                place[0] = place[0] + zr[d, i - 1, :blk].astype(F32)
                place[1] = place[1] + zr[d, i - 1, blk:].astype(F32)
        if k == 0:
            uin[...] = sums[0][0] / images + nin[...]
            uout[...] = sums[0][1] / images + nout[...]
            return
        for d in range(2):
            zs[d, i, :blk] = sums[d][0].astype(BF16)
            zs[d, i, blk:] = sums[d][1].astype(BF16)
        zc[i] = [
            send(zs.at[d, i], zr.at[d, i], z_send.at[d, i], z_recv.at[d, i], z_to[d])
            for d in range(2)
        ]

    g_copies = []

    def finish_input():
        for copy in x_copies:
            copy.wait_recv()
        at = pl.ds(pl.multiple_of(mp * rows, rows), rows)
        summed = part[at, :].astype(F32)
        for j in range(1, nmp):
            summed = summed + xrs[j].astype(F32)
        standardized, inverse, unused = layer_normalize(tok[at, :], gain[...], shift[...])
        scaled = summed * gain[...]
        difference = inverse * (
            scaled
            - jnp.mean(scaled, axis=-1, keepdims=True)
            - standardized * jnp.mean(scaled * standardized, axis=-1, keepdims=True)
        )
        ig[at, :] = (cot[at, :].astype(F32) + difference).astype(BF16)
        for j in range(1, nmp):
            g_copies.append(
                send(ig.at[at, :], ig.at[at, :], g_send.at[j], g_recv.at[j], (dp, at_mp(j)))
            )

    ahead = 3
    last = len(chunks)
    for i in range(min(ahead, last)):
        stage_a(i)
    for i in range(last):
        stage_b(i)
        if i + ahead < last:
            stage_a(i + ahead)
        if i > 0:
            stage_c(i - 1)
        if i == min(2, last - 1):
            finish_input()
    stage_c(last - 1)
    for copy in g_copies:
        copy.wait_recv()
    for copy in pending:
        copy.wait_send()


def per_device(nz, nmp, tokens, cotangent, gain, shift, w_in, w_out, noise_in, noise_out):
    seq, width = tokens.shape
    group = w_in.shape[1]
    blk = width // (NY * nz)
    rows = seq // nmp
    half = nz // 2
    vmem = pl.BlockSpec(memory_space=pltpu.VMEM)
    dma = pltpu.SemaphoreType.DMA
    input_grad, update_in, update_out = pl.pallas_call(
        functools.partial(kernel, nz, nmp),
        out_shape=(
            jax.ShapeDtypeStruct((seq, width), BF16),
            jax.ShapeDtypeStruct((blk, group), F32),
            jax.ShapeDtypeStruct((blk, group), F32),
        ),
        in_specs=[vmem] * 8,
        out_specs=(vmem,) * 3,
        scratch_shapes=[
            pltpu.VMEM((seq, width), BF16),
            pltpu.VMEM((seq, group), BF16),
            pltpu.VMEM((seq, group), BF16),
            pltpu.VMEM((seq, group), F32),
            pltpu.VMEM((seq, group), F32),
            pltpu.VMEM((width, group), F32),
            pltpu.VMEM((width, group), F32),
            pltpu.VMEM((seq, width), BF16),
            pltpu.VMEM((nmp, 8, 128), F32),
            pltpu.VMEM((nmp, rows, width), BF16),
            pltpu.VMEM((2, nz, blk, group), BF16),
            pltpu.VMEM((2, nz, blk, group), BF16),
            pltpu.VMEM((2, nz, 2 * blk, group), BF16),
            pltpu.VMEM((2, nz, 2 * blk, group), BF16),
            pltpu.VMEM((2, half, 2 * blk, group), BF16),
            pltpu.VMEM((2, half, 2 * blk, group), BF16),
            *[dma((nmp,))] * 6,
            *[dma((2, half + 1))] * 4,
            *[dma((2, half))] * 2,
        ],
        compiler_params=pltpu.CompilerParams(
            collective_id=0, has_side_effects=True, vmem_limit_bytes=48 * 1024 * 1024
        ),
    )(
        tokens, cotangent, gain.reshape(1, width), shift.reshape(1, width),
        w_in, w_out, noise_in, noise_out.T,
    )
    return input_grad, update_in, update_out.T


def solution(mesh):
    in_specs = (
        P("dp", None),
        P("dp", None),
        P(),
        P(),
        P(None, "mp"),
        P("mp", None),
        P("dp", "mp"),
        P("mp", "dp"),
    )
    out_specs = (P("dp", None), P("dp", "mp"), P("mp", "dp"))
    step = functools.partial(per_device, mesh.shape["dp"] // NY, mesh.shape["mp"])
    return jax.shard_map(
        step, mesh=mesh, in_specs=in_specs, out_specs=out_specs, check_vma=False
    )
```

```python
import functools
import math

import jax
import jax.numpy as jnp
from jax import lax
from jax.experimental import pallas as pl
from jax.experimental.pallas import tpu as pltpu
from jax.sharding import PartitionSpec as P

MESH = pl.DeviceIdType.MESH
NY = 4
B_AHEAD = 3
INPUT_AT = 3
FAR_AT = 6
BF16, F32 = jnp.bfloat16, jnp.float32


def layer_normalize(tokens, gain, shift):
    values = tokens.astype(F32)
    centered_rows = values - jnp.mean(values, axis=-1, keepdims=True)
    variance = jnp.mean(centered_rows * centered_rows, axis=-1, keepdims=True)
    inverse_deviation = lax.rsqrt(variance + 1e-05)
    standardized_input = centered_rows * inverse_deviation
    normalized_rows = (standardized_input * gain + shift).astype(BF16)
    return standardized_input, inverse_deviation, normalized_rows


def gelu_parts(pre):
    cumul = 0.5 * (1.0 + lax.erf(pre * (1.0 / math.sqrt(2.0))))
    density = jnp.exp(-0.5 * pre * pre) * (1.0 / math.sqrt(2.0 * math.pi))
    return pre * cumul, cumul + pre * density


def dot(left, right, dims):
    return lax.dot_general(left, right, (dims, ((), ())), preferred_element_type=F32)


def kernel(
    nz, nmp, *refs,
):
    hbm, rest = refs[:8], refs[8:]
    (
    ig, uin, uout,
    tok, cot, gain, shift, win, wout, nin, nout, in_sem,
    normed, act, grad, pre, back, pin, pout, part, nrm, xrs,
    s1, r1, s2, r2, zs, zr, acc,
    n_send, n_recv, x_send, x_recv, g_send, g_recv,
    y1_send, y1_recv, y2_send, y2_recv, z_send, z_recv,
    ) = rest
    local = (tok, cot, gain, shift, win, wout, nin, nout)
    loads = [
        pltpu.make_async_copy(src, dst, in_sem.at[i])
        for i, (src, dst) in enumerate(zip(hbm, local, strict=True))
    ]
    for i in (0, 2, 3, 4, 1, 5, 6, 7):
        loads[i].start()

    seq, width = tok.shape
    group = win.shape[1]
    blk = width // (NY * nz)
    rows = seq // nmp
    images = float(nz * NY)
    dp, mp = lax.axis_index("dp"), lax.axis_index("mp")
    z, y = lax.div(dp, NY), lax.rem(dp, NY)

    def at_y(step):
        return lax.rem(y + step + NY, NY)

    def at_z(step):
        return lax.rem(z + step + nz, nz)

    def at_mp(step):
        return lax.rem(mp + step, nmp)

    def far(dy, dz=0, j=0):
        return (at_z(dz) * NY + at_y(dy), at_mp(j))

    barrier = pltpu.get_barrier_semaphore()
    norm_to = [(dy, j) for dy in (0, 1, -1) for j in range(nmp) if dy != 0 or j != 0]
    greeted = [far(dy, 0, j) for dy, j in norm_to]
    greeted += [far(0, dz) for dz in (1, -1, 2, -2, 3, -3, 4, -4)]
    for other in greeted:
        pl.semaphore_signal(barrier, inc=1, device_id=other, device_id_type=MESH)

    pending = []

    def send(src, dst, send_sem, recv_sem, to):
        copy = pltpu.make_async_remote_copy(
            src_ref=src, dst_ref=dst, send_sem=send_sem, recv_sem=recv_sem,
            device_id=to, device_id_type=MESH,
        )
        copy.start()
        pending.append(copy)
        return copy

    tile = min(seq, 32)

    def norm_tile(t, carry):
        at = pl.ds(pl.multiple_of(t * tile, tile), tile)
        normed[at, :] = layer_normalize(tok[at, :], gain[...], shift[...])[2]
        return carry

    for i in (0, 2, 3):
        loads[i].wait()
    lax.fori_loop(0, seq // tile, norm_tile, 0)
    loads[4].wait()
    pre[...] = dot(normed[...], win[...], ((1,), (0,)))
    for i in (1, 5, 6, 7):
        loads[i].wait()
    back[...] = dot(cot[...], wout[...], ((1,), (1,)))

    def gelu_tile(t, carry):
        at = pl.ds(pl.multiple_of(t * tile, tile), tile)
        value, slope = gelu_parts(pre[at, :])
        act[at, :] = value.astype(BF16)
        grad[at, :] = (back[at, :] * slope).astype(BF16)
        return carry

    lax.fori_loop(0, seq // tile, gelu_tile, 0)

    step = min(width, 256)
    norm = jnp.zeros((8, 128), F32)
    for left, right, out in ((normed, grad, pin), (cot, act, pout)):
        for t in range(width // step):
            prod = dot(left[:, t * step : (t + 1) * step], right[...], ((0,), (0,)))
            out[t * step : (t + 1) * step, :] = prod
            square = jnp.sum((prod * prod).reshape(step // 8, 8, group), axis=0)
            for c in range(group // 128):
                norm = norm + square[:, c * 128 : (c + 1) * 128]
    nrm[0, 0] = norm

    chunks, first = [], 0
    for steps in ([8], [7, -7], [6, -6], [5, -5], [3, -3], [4, -4], [2, -2], [1, -1], [0]):
        chunks.append((first, steps))
        first += len(steps)
    y1, y2 = {}, {}

    def mine(which, dz, dy):
        at = pl.ds(pl.multiple_of((at_z(dz) * NY + at_y(dy)) * blk, blk), blk)
        return which[at, :]

    def stage_a(i):
        o, steps = chunks[i]
        for t, dz in enumerate(steps):
            s1[0, o + t] = mine(pin, dz, 2).astype(BF16)
            s1[1, o + t] = mine(pout, dz, 2).astype(BF16)
        at = pl.ds(o, len(steps))
        y1[i] = [
            send(s1.at[d, at], r1.at[d, at], y1_send.at[d, i], y1_recv.at[d, i], far(1 - 2 * d))
            for d in range(2)
        ]

    pl.semaphore_wait(barrier, len(greeted))
    n_copies = [
        send(nrm.at[0, 0], nrm.at[dy % 3, j], n_send.at[dy % 3, j], n_recv.at[dy % 3, j], far(dy, 0, j))
        for dy, j in norm_to
    ]
    for i in range(len(chunks)):
        stage_a(i)

    part[...] = dot(grad[...], win[...], ((1,), (1,))).astype(BF16)
    x_copies = []
    for j in range(1, nmp):
        at = pl.ds(pl.multiple_of(at_mp(j) * rows, rows), rows)
        x_copies.append(
            send(part.at[at, :], xrs.at[j], x_send.at[j], x_recv.at[j], far(0, 0, j))
        )

    for copy in n_copies:
        copy.wait_recv()

    def clip_of(k):
        total = jnp.sum(jnp.sum(nrm[k], axis=0), keepdims=True)
        return jnp.minimum(1.0, float(width) / jnp.sqrt(total + 1e-06))

    clip, clip_m, clip_p = clip_of(0), clip_of(1), clip_of(2)

    def stage_b(i):
        o, steps = chunks[i]
        for copy in y1[i]:
            copy.wait_recv()
        for t, dz in enumerate(steps):
            s = o + t
            s2[0, s, :blk] = (clip * mine(pin, dz, 1) + clip_m * r1[0, s].astype(F32)).astype(BF16)
            s2[0, s, blk:] = (clip * mine(pout, dz, 1)).astype(BF16)
            s2[1, s, :blk] = (clip * mine(pin, dz, -1)).astype(BF16)
            s2[1, s, blk:] = (clip * mine(pout, dz, -1) + clip_p * r1[1, s].astype(F32)).astype(BF16)
        at = pl.ds(o, len(steps))
        y2[i] = [
            send(s2.at[d, at], r2.at[d, at], y2_send.at[d, i], y2_recv.at[d, i], far(1 - 2 * d))
            for d in range(2)
        ]

    z_copies = {}
    hops = {3: -1, 5: 1, 6: 2, 7: 3, 8: 4}
    slot_of = {1: 0, 2: 1, 3: 4, 5: 5, 6: 6, 7: 7, 8: 8}

    def z_send_block(d, k, slot, hop, at):
        z_copies[d, k] = send(
            zs.at[d, slot, at], zr.at[d, slot, at], z_send.at[d, slot], z_recv.at[d, slot],
            far(0, hop if d == 0 else -hop),
        )

    whole = pl.ds(0, 2 * blk)

    def stage_c(i):
        o, steps = chunks[i]
        for copy in y2[i]:
            copy.wait_recv()
        for t, dz in enumerate(steps):
            s = o + t
            sums = [
                clip * mine(which, dz, 0) + r2[0, s, at].astype(F32) + r2[1, s, at].astype(F32)
                for which, at in ((pin, slice(0, blk)), (pout, slice(blk, 2 * blk)))
            ]
            k, d = abs(dz), 0 if dz >= 0 else 1
            if k == 0:
                return sums
            if k == 4:
                acc[d, :blk], acc[d, blk:] = sums
            elif k == 8:
                for d in range(2):
                    half = pl.ds(d * blk, blk)
                    zs[d, slot_of[8], half] = sums[d].astype(BF16)
                    z_send_block(d, 8, slot_of[8], 4, half)
            else:
                slot = slot_of[k]
                zs[d, slot, :blk] = sums[0].astype(BF16)
                zs[d, slot, blk:] = sums[1].astype(BF16)
                z_send_block(d, k, slot, hops.get(k, k), whole)

    def gather_far():
        for d in range(2):
            for k in (8, 7, 6, 5, 3):
                z_copies[d, k].wait_recv()
            half = pl.ds(d * blk, blk)
            acc[d, half] = acc[d, half] + zr[d, slot_of[8], half].astype(F32)
            total = acc[d]
            for k in (7, 6, 5, 3):
                total = total + zr[d, slot_of[k]].astype(F32)
            zs[d, 2] = total.astype(BF16)
            z_send_block(d, 4, 2, 4, whole)

    def finish_update(sums):
        for d in range(2):
            for k in (4, 2, 1):
                z_copies[d, k].wait_recv()
            for slot in (2, 1, 0):
                sums[0] = sums[0] + zr[d, slot, :blk].astype(F32)
                sums[1] = sums[1] + zr[d, slot, blk:].astype(F32)
        uin[...] = sums[0] / images + nin[...]
        uout[...] = sums[1] / images + nout[...]

    g_copies = []

    def finish_input():
        for copy in x_copies:
            copy.wait_recv()
        at = pl.ds(pl.multiple_of(mp * rows, rows), rows)
        summed = part[at, :].astype(F32)
        for j in range(1, nmp):
            summed = summed + xrs[j].astype(F32)
        standardized, inverse, unused = layer_normalize(tok[at, :], gain[...], shift[...])
        scaled = summed * gain[...]
        difference = inverse * (
            scaled
            - jnp.mean(scaled, axis=-1, keepdims=True)
            - standardized * jnp.mean(scaled * standardized, axis=-1, keepdims=True)
        )
        ig[at, :] = (cot[at, :].astype(F32) + difference).astype(BF16)
        for j in range(1, nmp):
            g_copies.append(
                send(ig.at[at, :], ig.at[at, :], g_send.at[j], g_recv.at[j], (dp, at_mp(j)))
            )

    last = len(chunks)
    for i in range(last + B_AHEAD):
        if i < last:
            stage_b(i)
        if i >= B_AHEAD:
            sums = stage_c(i - B_AHEAD)
            if i - B_AHEAD == INPUT_AT:
                finish_input()
            if i - B_AHEAD == FAR_AT:
                gather_far()
    finish_update(sums)
    for copy in g_copies:
        copy.wait_recv()
    for copy in pending:
        copy.wait_send()


def per_device(nz, nmp, tokens, cotangent, gain, shift, w_in, w_out, noise_in, noise_out):
    seq, width = tokens.shape
    group = w_in.shape[1]
    blk = width // (NY * nz)
    rows = seq // nmp
    vmem = pl.BlockSpec(memory_space=pltpu.VMEM)
    dma = pltpu.SemaphoreType.DMA
    input_grad, update_in, update_out = pl.pallas_call(
        functools.partial(kernel, nz, nmp),
        out_shape=(
            jax.ShapeDtypeStruct((seq, width), BF16),
            jax.ShapeDtypeStruct((blk, group), F32),
            jax.ShapeDtypeStruct((blk, group), F32),
        ),
        in_specs=[pl.BlockSpec(memory_space=pltpu.HBM)] * 8,
        out_specs=(vmem,) * 3,
        scratch_shapes=[
            pltpu.VMEM((seq, width), BF16),
            pltpu.VMEM((seq, width), BF16),
            pltpu.VMEM((1, width), F32),
            pltpu.VMEM((1, width), F32),
            pltpu.VMEM((width, group), BF16),
            pltpu.VMEM((group, width), BF16),
            pltpu.VMEM((blk, group), F32),
            pltpu.VMEM((blk, group), F32),
            dma((8,)),
            pltpu.VMEM((seq, width), BF16),
            pltpu.VMEM((seq, group), BF16),
            pltpu.VMEM((seq, group), BF16),
            pltpu.VMEM((seq, group), F32),
            pltpu.VMEM((seq, group), F32),
            pltpu.VMEM((width, group), F32),
            pltpu.VMEM((width, group), F32),
            pltpu.VMEM((seq, width), BF16),
            pltpu.VMEM((3, nmp, 8, 128), F32),
            pltpu.VMEM((nmp, rows, width), BF16),
            pltpu.VMEM((2, nz, blk, group), BF16),
            pltpu.VMEM((2, nz, blk, group), BF16),
            pltpu.VMEM((2, nz, 2 * blk, group), BF16),
            pltpu.VMEM((2, nz, 2 * blk, group), BF16),
            pltpu.VMEM((2, 9, 2 * blk, group), BF16),
            pltpu.VMEM((2, 9, 2 * blk, group), BF16),
            pltpu.VMEM((2, 2 * blk, group), F32),
            *[dma((3, nmp))] * 2,
            *[dma((nmp,))] * 4,
            *[dma((2, 9))] * 6,
        ],
        compiler_params=pltpu.CompilerParams(
            collective_id=0, has_side_effects=True, vmem_limit_bytes=64 * 1024 * 1024
        ),
    )(
        tokens, cotangent, gain.reshape(1, width), shift.reshape(1, width),
        w_in, w_out, noise_in, noise_out.T,
    )
    return input_grad, update_in, update_out.T


def solution(mesh):
    in_specs = (
        P("dp", None),
        P("dp", None),
        P(),
        P(),
        P(None, "mp"),
        P("mp", None),
        P("dp", "mp"),
        P("mp", "dp"),
    )
    out_specs = (P("dp", None), P("dp", "mp"), P("mp", "dp"))
    step = functools.partial(per_device, mesh.shape["dp"] // NY, mesh.shape["mp"])
    return jax.shard_map(
        step, mesh=mesh, in_specs=in_specs, out_specs=out_specs, check_vma=False
    )
```

```python
import functools
import math

import jax
import jax.numpy as jnp
from jax import lax
from jax.experimental import pallas as pl
from jax.experimental.pallas import tpu as pltpu
from jax.sharding import PartitionSpec as P

MESH = pl.DeviceIdType.MESH
NY = 4
B_AHEAD = 3
INPUT_AT = 3
FAR_AT = 6
BF16, F32 = jnp.bfloat16, jnp.float32


def layer_normalize(tokens, gain, shift):
    values = tokens.astype(F32)
    centered_rows = values - jnp.mean(values, axis=-1, keepdims=True)
    variance = jnp.mean(centered_rows * centered_rows, axis=-1, keepdims=True)
    inverse_deviation = lax.rsqrt(variance + 1e-05)
    standardized_input = centered_rows * inverse_deviation
    normalized_rows = (standardized_input * gain + shift).astype(BF16)
    return standardized_input, inverse_deviation, normalized_rows


def gelu_parts(pre):
    cumul = 0.5 * (1.0 + lax.erf(pre * (1.0 / math.sqrt(2.0))))
    density = jnp.exp(-0.5 * pre * pre) * (1.0 / math.sqrt(2.0 * math.pi))
    return pre * cumul, cumul + pre * density


def dot(left, right, dims):
    return lax.dot_general(left, right, (dims, ((), ())), preferred_element_type=F32)


def kernel(
    nz, nmp, *refs,
):
    hbm, rest = refs[:8], refs[8:]
    (
    ig, uin, uout,
    tok, cot, gain, shift, win, wout, nin, nout, in_sem,
    normed, act, grad, pre, back, pin, pout, part, nrm, xrs,
    s1, r1, s2, r2, zs, zr, acc,
    n_send, n_recv, x_send, x_recv, g_send, g_recv,
    y1_send, y1_recv, y2_send, y2_recv, z_send, z_recv,
    ) = rest
    local = (tok, cot, gain, shift, win, wout, nin, nout)
    loads = [
        pltpu.make_async_copy(src, dst, in_sem.at[i])
        for i, (src, dst) in enumerate(zip(hbm, local, strict=True))
    ]
    for i in (0, 2, 3, 4, 1, 5, 6, 7):
        loads[i].start()

    seq, width = tok.shape
    group = win.shape[1]
    blk = width // (NY * nz)
    rows = seq // nmp
    images = float(nz * NY)
    dp, mp = lax.axis_index("dp"), lax.axis_index("mp")
    z, y = lax.div(dp, NY), lax.rem(dp, NY)

    def at_y(step):
        return lax.rem(y + step + NY, NY)

    def at_z(step):
        return lax.rem(z + step + nz, nz)

    def at_mp(step):
        return lax.rem(mp + step, nmp)

    def far(dy, dz=0, j=0):
        return (at_z(dz) * NY + at_y(dy), at_mp(j))

    barrier = pltpu.get_barrier_semaphore()
    norm_to = [(dy, j) for dy in (0, 1, -1) for j in range(nmp) if dy != 0 or j != 0]
    greeted = [far(dy, 0, j) for dy, j in norm_to]
    greeted += [far(0, dz) for dz in (1, -1, 2, -2, 3, -3, 4, -4)]
    for other in greeted:
        pl.semaphore_signal(barrier, inc=1, device_id=other, device_id_type=MESH)

    pending = []

    def send(src, dst, send_sem, recv_sem, to):
        copy = pltpu.make_async_remote_copy(
            src_ref=src, dst_ref=dst, send_sem=send_sem, recv_sem=recv_sem,
            device_id=to, device_id_type=MESH,
        )
        copy.start()
        pending.append(copy)
        return copy

    tile = min(seq, 32)

    def norm_tile(t, carry):
        at = pl.ds(pl.multiple_of(t * tile, tile), tile)
        normed[at, :] = layer_normalize(tok[at, :], gain[...], shift[...])[2]
        return carry

    for i in (0, 2, 3):
        loads[i].wait()
    lax.fori_loop(0, seq // tile, norm_tile, 0)
    loads[4].wait()
    pre[...] = dot(normed[...], win[...], ((1,), (0,)))
    for i in (1, 5, 6, 7):
        loads[i].wait()
    back[...] = dot(cot[...], wout[...], ((1,), (1,)))

    def gelu_tile(t, carry):
        at = pl.ds(pl.multiple_of(t * tile, tile), tile)
        value, slope = gelu_parts(pre[at, :])
        act[at, :] = value.astype(BF16)
        grad[at, :] = (back[at, :] * slope).astype(BF16)
        return carry

    lax.fori_loop(0, seq // tile, gelu_tile, 0)

    step = min(width, 256)
    norm = jnp.zeros((8, 128), F32)
    for left, right, out in ((normed, grad, pin), (cot, act, pout)):
        for t in range(width // step):
            prod = dot(left[:, t * step : (t + 1) * step], right[...], ((0,), (0,)))
            out[t * step : (t + 1) * step, :] = prod
            square = jnp.sum((prod * prod).reshape(step // 8, 8, group), axis=0)
            for c in range(group // 128):
                norm = norm + square[:, c * 128 : (c + 1) * 128]
    nrm[0, 0] = norm

    chunks, first = [], 0
    for steps in ([8], [7, -7], [6, -6], [5, -5], [3, -3], [4, -4], [2, -2], [1, -1], [0]):
        chunks.append((first, steps))
        first += len(steps)
    y1, y2 = {}, {}

    def mine(which, dz, dy):
        at = pl.ds(pl.multiple_of((at_z(dz) * NY + at_y(dy)) * blk, blk), blk)
        return which[at, :]

    def stage_a(i):
        o, steps = chunks[i]
        for t, dz in enumerate(steps):
            s1[0, o + t] = mine(pin, dz, 2).astype(BF16)
            s1[1, o + t] = mine(pout, dz, 2).astype(BF16)
        at = pl.ds(o, len(steps))
        y1[i] = [
            send(s1.at[d, at], r1.at[d, at], y1_send.at[d, i], y1_recv.at[d, i], far(1 - 2 * d))
            for d in range(2)
        ]

    pl.semaphore_wait(barrier, len(greeted))
    n_copies = [
        send(nrm.at[0, 0], nrm.at[dy % 3, j], n_send.at[dy % 3, j], n_recv.at[dy % 3, j], far(dy, 0, j))
        for dy, j in norm_to
    ]
    for i in range(len(chunks)):
        stage_a(i)

    part[...] = dot(grad[...], win[...], ((1,), (1,))).astype(BF16)
    x_copies = []
    for j in range(1, nmp):
        at = pl.ds(pl.multiple_of(at_mp(j) * rows, rows), rows)
        x_copies.append(
            send(part.at[at, :], xrs.at[j], x_send.at[j], x_recv.at[j], far(0, 0, j))
        )

    for copy in n_copies:
        copy.wait_recv()

    def clip_of(k):
        total = jnp.sum(jnp.sum(nrm[k], axis=0), keepdims=True)
        return jnp.minimum(1.0, float(width) / jnp.sqrt(total + 1e-06))

    clip, clip_m, clip_p = clip_of(0), clip_of(1), clip_of(2)

    def stage_b(i):
        o, steps = chunks[i]
        for copy in y1[i]:
            copy.wait_recv()
        for t, dz in enumerate(steps):
            s = o + t
            s2[0, s, :blk] = (clip * mine(pin, dz, 1) + clip_m * r1[0, s].astype(F32)).astype(BF16)
            s2[0, s, blk:] = (clip * mine(pout, dz, 1)).astype(BF16)
            s2[1, s, :blk] = (clip * mine(pin, dz, -1)).astype(BF16)
            s2[1, s, blk:] = (clip * mine(pout, dz, -1) + clip_p * r1[1, s].astype(F32)).astype(BF16)
        at = pl.ds(o, len(steps))
        y2[i] = [
            send(s2.at[d, at], r2.at[d, at], y2_send.at[d, i], y2_recv.at[d, i], far(1 - 2 * d))
            for d in range(2)
        ]

    z_copies = {}
    hops = {3: -1, 5: 1, 6: 2, 7: 3, 8: 4}
    slot_of = {1: 0, 2: 1, 3: 4, 5: 5, 6: 6, 7: 7, 8: 8}

    def z_send_block(d, k, slot, hop, at):
        z_copies[d, k] = send(
            zs.at[d, slot, at], zr.at[d, slot, at], z_send.at[d, slot], z_recv.at[d, slot],
            far(0, hop if d == 0 else -hop),
        )

    whole = pl.ds(0, 2 * blk)

    def stage_c(i):
        o, steps = chunks[i]
        for copy in y2[i]:
            copy.wait_recv()
        for t, dz in enumerate(steps):
            s = o + t
            sums = [
                clip * mine(which, dz, 0) + r2[0, s, at].astype(F32) + r2[1, s, at].astype(F32)
                for which, at in ((pin, slice(0, blk)), (pout, slice(blk, 2 * blk)))
            ]
            k, d = abs(dz), 0 if dz >= 0 else 1
            if k == 0:
                return sums
            if k == 4:
                acc[d, :blk], acc[d, blk:] = sums
            elif k == 8:
                for d in range(2):
                    half = pl.ds(d * blk, blk)
                    zs[d, slot_of[8], half] = sums[d].astype(BF16)
                    z_send_block(d, 8, slot_of[8], 4, half)
            else:
                slot = slot_of[k]
                zs[d, slot, :blk] = sums[0].astype(BF16)
                zs[d, slot, blk:] = sums[1].astype(BF16)
                z_send_block(d, k, slot, hops.get(k, k), whole)

    def gather_far():
        for d in range(2):
            for k in (8, 7, 6, 5, 3):
                z_copies[d, k].wait_recv()
            half = pl.ds(d * blk, blk)
            acc[d, half] = acc[d, half] + zr[d, slot_of[8], half].astype(F32)
            total = acc[d]
            for k in (7, 6, 5, 3):
                total = total + zr[d, slot_of[k]].astype(F32)
            zs[d, 2] = total.astype(BF16)
            z_send_block(d, 4, 2, 4, whole)

    def finish_update(sums):
        for copy in pending:
            copy.wait_send()
        pending.clear()
        for d in range(2):
            for k in (4, 2, 1):
                z_copies[d, k].wait_recv()
            for slot in (2, 1, 0):
                sums[0] = sums[0] + zr[d, slot, :blk].astype(F32)
                sums[1] = sums[1] + zr[d, slot, blk:].astype(F32)
        uin[...] = sums[0] / images + nin[...]
        uout[...] = sums[1] / images + nout[...]

    g_copies = []

    def finish_input():
        for copy in x_copies:
            copy.wait_recv()
        at = pl.ds(pl.multiple_of(mp * rows, rows), rows)
        summed = part[at, :].astype(F32)
        for j in range(1, nmp):
            summed = summed + xrs[j].astype(F32)
        standardized, inverse, unused = layer_normalize(tok[at, :], gain[...], shift[...])
        scaled = summed * gain[...]
        difference = inverse * (
            scaled
            - jnp.mean(scaled, axis=-1, keepdims=True)
            - standardized * jnp.mean(scaled * standardized, axis=-1, keepdims=True)
        )
        ig[at, :] = (cot[at, :].astype(F32) + difference).astype(BF16)
        for j in range(1, nmp):
            g_copies.append(
                send(ig.at[at, :], ig.at[at, :], g_send.at[j], g_recv.at[j], (dp, at_mp(j)))
            )

    last = len(chunks)
    for i in range(last + B_AHEAD):
        if i < last:
            stage_b(i)
        if i >= B_AHEAD:
            sums = stage_c(i - B_AHEAD)
            if i - B_AHEAD == INPUT_AT:
                finish_input()
            if i - B_AHEAD == FAR_AT:
                gather_far()
    finish_update(sums)
    for copy in g_copies:
        copy.wait_recv()
    for copy in pending:
        copy.wait_send()


def per_device(nz, nmp, tokens, cotangent, gain, shift, w_in, w_out, noise_in, noise_out):
    seq, width = tokens.shape
    group = w_in.shape[1]
    blk = width // (NY * nz)
    rows = seq // nmp
    vmem = pl.BlockSpec(memory_space=pltpu.VMEM)
    dma = pltpu.SemaphoreType.DMA
    input_grad, update_in, update_out = pl.pallas_call(
        functools.partial(kernel, nz, nmp),
        out_shape=(
            jax.ShapeDtypeStruct((seq, width), BF16),
            jax.ShapeDtypeStruct((blk, group), F32),
            jax.ShapeDtypeStruct((blk, group), F32),
        ),
        in_specs=[pl.BlockSpec(memory_space=pltpu.HBM)] * 8,
        out_specs=(vmem,) * 3,
        scratch_shapes=[
            pltpu.VMEM((seq, width), BF16),
            pltpu.VMEM((seq, width), BF16),
            pltpu.VMEM((1, width), F32),
            pltpu.VMEM((1, width), F32),
            pltpu.VMEM((width, group), BF16),
            pltpu.VMEM((group, width), BF16),
            pltpu.VMEM((blk, group), F32),
            pltpu.VMEM((blk, group), F32),
            dma((8,)),
            pltpu.VMEM((seq, width), BF16),
            pltpu.VMEM((seq, group), BF16),
            pltpu.VMEM((seq, group), BF16),
            pltpu.VMEM((seq, group), F32),
            pltpu.VMEM((seq, group), F32),
            pltpu.VMEM((width, group), F32),
            pltpu.VMEM((width, group), F32),
            pltpu.VMEM((seq, width), BF16),
            pltpu.VMEM((3, nmp, 8, 128), F32),
            pltpu.VMEM((nmp, rows, width), BF16),
            pltpu.VMEM((2, nz, blk, group), BF16),
            pltpu.VMEM((2, nz, blk, group), BF16),
            pltpu.VMEM((2, nz, 2 * blk, group), BF16),
            pltpu.VMEM((2, nz, 2 * blk, group), BF16),
            pltpu.VMEM((2, 9, 2 * blk, group), BF16),
            pltpu.VMEM((2, 9, 2 * blk, group), BF16),
            pltpu.VMEM((2, 2 * blk, group), F32),
            *[dma((3, nmp))] * 2,
            *[dma((nmp,))] * 4,
            *[dma((2, 9))] * 6,
        ],
        compiler_params=pltpu.CompilerParams(
            collective_id=0, has_side_effects=True, vmem_limit_bytes=64 * 1024 * 1024
        ),
    )(
        tokens, cotangent, gain.reshape(1, width), shift.reshape(1, width),
        w_in, w_out, noise_in, noise_out.T,
    )
    return input_grad, update_in, update_out.T


def solution(mesh):
    in_specs = (
        P("dp", None),
        P("dp", None),
        P(),
        P(),
        P(None, "mp"),
        P("mp", None),
        P("dp", "mp"),
        P("mp", "dp"),
    )
    out_specs = (P("dp", None), P("dp", "mp"), P("mp", "dp"))
    step = functools.partial(per_device, mesh.shape["dp"] // NY, mesh.shape["mp"])
    return jax.shard_map(
        step, mesh=mesh, in_specs=in_specs, out_specs=out_specs, check_vma=False
    )
```

```python
import functools
import math

import jax
import jax.numpy as jnp
from jax import lax
from jax.experimental import pallas as pl
from jax.experimental.pallas import tpu as pltpu
from jax.sharding import PartitionSpec as P

MESH = pl.DeviceIdType.MESH
NY = 4
B_AHEAD = 3
INPUT_AT = 3
FAR_AT = 6
BF16, F32 = jnp.bfloat16, jnp.float32


def layer_normalize(tokens, gain, shift):
    values = tokens.astype(F32)
    centered_rows = values - jnp.mean(values, axis=-1, keepdims=True)
    variance = jnp.mean(centered_rows * centered_rows, axis=-1, keepdims=True)
    inverse_deviation = lax.rsqrt(variance + 1e-05)
    standardized_input = centered_rows * inverse_deviation
    normalized_rows = (standardized_input * gain + shift).astype(BF16)
    return standardized_input, inverse_deviation, normalized_rows


def gelu_parts(pre):
    cumul = 0.5 * (1.0 + lax.erf(pre * (1.0 / math.sqrt(2.0))))
    density = jnp.exp(-0.5 * pre * pre) * (1.0 / math.sqrt(2.0 * math.pi))
    return pre * cumul, cumul + pre * density


def dot(left, right, dims):
    return lax.dot_general(left, right, (dims, ((), ())), preferred_element_type=F32)


def kernel(
    nz, nmp, *refs,
):
    hbm, rest = refs[:8], refs[8:]
    (
    ig, uin, uout,
    tok, cot, gain, shift, win, wout, nin, nout, in_sem,
    normed, act, grad, pre, back, pin, pout, part, nrm, xrs,
    igv, out_sem, s1, r1, s2, r2, zs, zr, acc,
    n_send, n_recv, x_send, x_recv, g_send, g_recv,
    y1_send, y1_recv, y2_send, y2_recv, z_send, z_recv,
    ) = rest
    local = (tok, cot, gain, shift, win, wout, nin, nout)
    loads = [
        pltpu.make_async_copy(src, dst, in_sem.at[i])
        for i, (src, dst) in enumerate(zip(hbm, local, strict=True))
    ]
    for i in (0, 2, 3, 4, 1, 5, 6, 7):
        loads[i].start()

    seq, width = tok.shape
    group = win.shape[1]
    blk = width // (NY * nz)
    rows = seq // nmp
    images = float(nz * NY)
    dp, mp = lax.axis_index("dp"), lax.axis_index("mp")
    z, y = lax.div(dp, NY), lax.rem(dp, NY)

    def at_y(step):
        return lax.rem(y + step + NY, NY)

    def at_z(step):
        return lax.rem(z + step + nz, nz)

    def at_mp(step):
        return lax.rem(mp + step, nmp)

    def far(dy, dz=0, j=0):
        return (at_z(dz) * NY + at_y(dy), at_mp(j))

    barrier = pltpu.get_barrier_semaphore()
    norm_to = [(dy, j) for dy in (0, 1, -1) for j in range(nmp) if dy != 0 or j != 0]
    greeted = [far(dy, 0, j) for dy, j in norm_to]
    greeted += [far(0, dz) for dz in (1, -1, 2, -2, 3, -3, 4, -4)]
    for other in greeted:
        pl.semaphore_signal(barrier, inc=1, device_id=other, device_id_type=MESH)

    pending = []

    def send(src, dst, send_sem, recv_sem, to):
        copy = pltpu.make_async_remote_copy(
            src_ref=src, dst_ref=dst, send_sem=send_sem, recv_sem=recv_sem,
            device_id=to, device_id_type=MESH,
        )
        copy.start()
        pending.append(copy)
        return copy

    tile = min(seq, 32)

    def norm_tile(t, carry):
        at = pl.ds(pl.multiple_of(t * tile, tile), tile)
        normed[at, :] = layer_normalize(tok[at, :], gain[...], shift[...])[2]
        return carry

    for i in (0, 2, 3):
        loads[i].wait()
    lax.fori_loop(0, seq // tile, norm_tile, 0)
    loads[4].wait()
    pre[...] = dot(normed[...], win[...], ((1,), (0,)))
    for i in (1, 5, 6, 7):
        loads[i].wait()
    back[...] = dot(cot[...], wout[...], ((1,), (1,)))

    def gelu_tile(t, carry):
        at = pl.ds(pl.multiple_of(t * tile, tile), tile)
        value, slope = gelu_parts(pre[at, :])
        act[at, :] = value.astype(BF16)
        grad[at, :] = (back[at, :] * slope).astype(BF16)
        return carry

    lax.fori_loop(0, seq // tile, gelu_tile, 0)

    step = min(width, 256)
    norm = jnp.zeros((8, 128), F32)
    for left, right, out in ((normed, grad, pin), (cot, act, pout)):
        for t in range(width // step):
            prod = dot(left[:, t * step : (t + 1) * step], right[...], ((0,), (0,)))
            out[t * step : (t + 1) * step, :] = prod
            square = jnp.sum((prod * prod).reshape(step // 8, 8, group), axis=0)
            for c in range(group // 128):
                norm = norm + square[:, c * 128 : (c + 1) * 128]
    nrm[0, 0] = norm

    chunks, first = [], 0
    for steps in ([8], [7, -7], [6, -6], [5, -5], [3, -3], [4, -4], [2, -2], [1, -1], [0]):
        chunks.append((first, steps))
        first += len(steps)
    y1, y2 = {}, {}

    def mine(which, dz, dy):
        at = pl.ds(pl.multiple_of((at_z(dz) * NY + at_y(dy)) * blk, blk), blk)
        return which[at, :]

    def stage_a(i):
        o, steps = chunks[i]
        for t, dz in enumerate(steps):
            s1[0, o + t] = mine(pin, dz, 2).astype(BF16)
            s1[1, o + t] = mine(pout, dz, 2).astype(BF16)
        at = pl.ds(o, len(steps))
        y1[i] = [
            send(s1.at[d, at], r1.at[d, at], y1_send.at[d, i], y1_recv.at[d, i], far(1 - 2 * d))
            for d in range(2)
        ]

    pl.semaphore_wait(barrier, len(greeted))
    n_copies = [
        send(nrm.at[0, 0], nrm.at[dy % 3, j], n_send.at[dy % 3, j], n_recv.at[dy % 3, j], far(dy, 0, j))
        for dy, j in norm_to
    ]
    for i in range(len(chunks)):
        stage_a(i)

    part[...] = dot(grad[...], win[...], ((1,), (1,))).astype(BF16)
    x_copies = []
    for j in range(1, nmp):
        at = pl.ds(pl.multiple_of(at_mp(j) * rows, rows), rows)
        x_copies.append(
            send(part.at[at, :], xrs.at[j], x_send.at[j], x_recv.at[j], far(0, 0, j))
        )

    for copy in n_copies:
        copy.wait_recv()

    def clip_of(k):
        total = jnp.sum(jnp.sum(nrm[k], axis=0), keepdims=True)
        return jnp.minimum(1.0, float(width) / jnp.sqrt(total + 1e-06))

    clip, clip_m, clip_p = clip_of(0), clip_of(1), clip_of(2)

    def stage_b(i):
        o, steps = chunks[i]
        for copy in y1[i]:
            copy.wait_recv()
        for t, dz in enumerate(steps):
            s = o + t
            s2[0, s, :blk] = (clip * mine(pin, dz, 1) + clip_m * r1[0, s].astype(F32)).astype(BF16)
            s2[0, s, blk:] = (clip * mine(pout, dz, 1)).astype(BF16)
            s2[1, s, :blk] = (clip * mine(pin, dz, -1)).astype(BF16)
            s2[1, s, blk:] = (clip * mine(pout, dz, -1) + clip_p * r1[1, s].astype(F32)).astype(BF16)
        at = pl.ds(o, len(steps))
        y2[i] = [
            send(s2.at[d, at], r2.at[d, at], y2_send.at[d, i], y2_recv.at[d, i], far(1 - 2 * d))
            for d in range(2)
        ]

    z_copies = {}
    hops = {3: -1, 5: 1, 6: 2, 7: 3, 8: 4}
    slot_of = {1: 0, 2: 1, 3: 4, 5: 5, 6: 6, 7: 7, 8: 8}

    def z_send_block(d, k, slot, hop, at):
        z_copies[d, k] = send(
            zs.at[d, slot, at], zr.at[d, slot, at], z_send.at[d, slot], z_recv.at[d, slot],
            far(0, hop if d == 0 else -hop),
        )

    whole = pl.ds(0, 2 * blk)

    def stage_c(i):
        o, steps = chunks[i]
        for copy in y2[i]:
            copy.wait_recv()
        for t, dz in enumerate(steps):
            s = o + t
            sums = [
                clip * mine(which, dz, 0) + r2[0, s, at].astype(F32) + r2[1, s, at].astype(F32)
                for which, at in ((pin, slice(0, blk)), (pout, slice(blk, 2 * blk)))
            ]
            k, d = abs(dz), 0 if dz >= 0 else 1
            if k == 0:
                return sums
            if k == 4:
                acc[d, :blk], acc[d, blk:] = sums
            elif k == 8:
                for d in range(2):
                    half = pl.ds(d * blk, blk)
                    zs[d, slot_of[8], half] = sums[d].astype(BF16)
                    z_send_block(d, 8, slot_of[8], 4, half)
            else:
                slot = slot_of[k]
                zs[d, slot, :blk] = sums[0].astype(BF16)
                zs[d, slot, blk:] = sums[1].astype(BF16)
                z_send_block(d, k, slot, hops.get(k, k), whole)

    def gather_far():
        for d in range(2):
            for k in (8, 7, 6, 5, 3):
                z_copies[d, k].wait_recv()
            half = pl.ds(d * blk, blk)
            acc[d, half] = acc[d, half] + zr[d, slot_of[8], half].astype(F32)
            total = acc[d]
            for k in (7, 6, 5, 3):
                total = total + zr[d, slot_of[k]].astype(F32)
            zs[d, 2] = total.astype(BF16)
            z_send_block(d, 4, 2, 4, whole)

    def finish_update(sums):
        for copy in pending:
            copy.wait_send()
        pending.clear()
        for d in range(2):
            for k in (4, 2, 1):
                z_copies[d, k].wait_recv()
            for slot in (2, 1, 0):
                sums[0] = sums[0] + zr[d, slot, :blk].astype(F32)
                sums[1] = sums[1] + zr[d, slot, blk:].astype(F32)
        uin[...] = sums[0] / images + nin[...]
        uout[...] = sums[1] / images + nout[...]

    g_copies = []

    def finish_input():
        for copy in x_copies:
            copy.wait_recv()
        at = pl.ds(pl.multiple_of(mp * rows, rows), rows)
        summed = part[at, :].astype(F32)
        for j in range(1, nmp):
            summed = summed + xrs[j].astype(F32)
        standardized, inverse, unused = layer_normalize(tok[at, :], gain[...], shift[...])
        scaled = summed * gain[...]
        difference = inverse * (
            scaled
            - jnp.mean(scaled, axis=-1, keepdims=True)
            - standardized * jnp.mean(scaled * standardized, axis=-1, keepdims=True)
        )
        igv[at, :] = (cot[at, :].astype(F32) + difference).astype(BF16)
        for j in range(1, nmp):
            g_copies.append(
                send(igv.at[at, :], igv.at[at, :], g_send.at[j], g_recv.at[j], (dp, at_mp(j)))
            )

    last = len(chunks)
    for i in range(last + B_AHEAD):
        if i < last:
            stage_b(i)
        if i >= B_AHEAD:
            sums = stage_c(i - B_AHEAD)
            if i - B_AHEAD == INPUT_AT:
                finish_input()
            if i - B_AHEAD == FAR_AT:
                gather_far()
    for copy in g_copies:
        copy.wait_recv()
    store = pltpu.make_async_copy(igv, ig, out_sem)
    store.start()
    finish_update(sums)
    store.wait()
    for copy in pending:
        copy.wait_send()


def per_device(nz, nmp, tokens, cotangent, gain, shift, w_in, w_out, noise_in, noise_out):
    seq, width = tokens.shape
    group = w_in.shape[1]
    blk = width // (NY * nz)
    rows = seq // nmp
    vmem = pl.BlockSpec(memory_space=pltpu.VMEM)
    dma = pltpu.SemaphoreType.DMA
    input_grad, update_in, update_out = pl.pallas_call(
        functools.partial(kernel, nz, nmp),
        out_shape=(
            jax.ShapeDtypeStruct((seq, width), BF16),
            jax.ShapeDtypeStruct((blk, group), F32),
            jax.ShapeDtypeStruct((blk, group), F32),
        ),
        in_specs=[pl.BlockSpec(memory_space=pltpu.HBM)] * 8,
        out_specs=(pl.BlockSpec(memory_space=pltpu.HBM), vmem, vmem),
        scratch_shapes=[
            pltpu.VMEM((seq, width), BF16),
            pltpu.VMEM((seq, width), BF16),
            pltpu.VMEM((1, width), F32),
            pltpu.VMEM((1, width), F32),
            pltpu.VMEM((width, group), BF16),
            pltpu.VMEM((group, width), BF16),
            pltpu.VMEM((blk, group), F32),
            pltpu.VMEM((blk, group), F32),
            dma((8,)),
            pltpu.VMEM((seq, width), BF16),
            pltpu.VMEM((seq, group), BF16),
            pltpu.VMEM((seq, group), BF16),
            pltpu.VMEM((seq, group), F32),
            pltpu.VMEM((seq, group), F32),
            pltpu.VMEM((width, group), F32),
            pltpu.VMEM((width, group), F32),
            pltpu.VMEM((seq, width), BF16),
            pltpu.VMEM((3, nmp, 8, 128), F32),
            pltpu.VMEM((nmp, rows, width), BF16),
            pltpu.VMEM((seq, width), BF16),
            dma,
            pltpu.VMEM((2, nz, blk, group), BF16),
            pltpu.VMEM((2, nz, blk, group), BF16),
            pltpu.VMEM((2, nz, 2 * blk, group), BF16),
            pltpu.VMEM((2, nz, 2 * blk, group), BF16),
            pltpu.VMEM((2, 9, 2 * blk, group), BF16),
            pltpu.VMEM((2, 9, 2 * blk, group), BF16),
            pltpu.VMEM((2, 2 * blk, group), F32),
            *[dma((3, nmp))] * 2,
            *[dma((nmp,))] * 4,
            *[dma((2, 9))] * 6,
        ],
        compiler_params=pltpu.CompilerParams(
            collective_id=0, has_side_effects=True, vmem_limit_bytes=64 * 1024 * 1024
        ),
    )(
        tokens, cotangent, gain.reshape(1, width), shift.reshape(1, width),
        w_in, w_out, noise_in, noise_out.T,
    )
    return input_grad, update_in, update_out.T


def solution(mesh):
    in_specs = (
        P("dp", None),
        P("dp", None),
        P(),
        P(),
        P(None, "mp"),
        P("mp", None),
        P("dp", "mp"),
        P("mp", "dp"),
    )
    out_specs = (P("dp", None), P("dp", "mp"), P("mp", "dp"))
    step = functools.partial(per_device, mesh.shape["dp"] // NY, mesh.shape["mp"])
    return jax.shard_map(
        step, mesh=mesh, in_specs=in_specs, out_specs=out_specs, check_vma=False
    )
```
